32 devices in a mesh: rows: 4 (over z), cols: 2 (over y), layers: 4 (over x, core).
Axes of the slice: x: 2, y: 2, z: 4, core: 2. Of those that a mesh axis runs over, the one named last changes fastest.
Arguments:
- bottom_known_vector: float32 [192, 128, 256], P(('rows', 'layers')), may hold values from -6 to 6
- bottom_pivot_reciprocal: float32 [192, 128, 128], P(('rows', 'layers'), 'cols'), as said below
- leaf_blocks: float32 [192, 2, 128, 128], P(('rows', 'layers'), 'cols'), may hold values from -0.0546875 to 0.0546875
- leaf_target: int32 [192, 2], P(('rows', 'layers'), 'cols'), may hold values from 0 to 3, as said below
- top_rhs: float32 [4, 128, 256], P('rows'), may hold values from -6 to 6
- top_inv: float32 [4, 128, 128], P('rows'), as said below
- top_sub: float32 [4, 128, 128], P('rows'), may hold values from -0.4375 to 0.4375
Outputs:
- leaf_solution: float32 [192, 128, 256], P(('rows', 'layers'), 'cols')
- top_solution: float32 [4, 128, 256], P('rows')
The draws below stay inside these ranges and needn't reach their ends.
Inputs may be any that keep to these rules, and one draw needn't show every extreme that they name: `leaf_target`: each leaf names 2 different top supernodes. `bottom_pivot_reciprocal`: each block is its diagonal times a factor of 0.7 to 1.3 plus a full-rank off-diagonal part. `top_inv`: each block is its diagonal times a factor of 0.7 to 1.3 plus a full-rank off-diagonal part.
All inputs are finite; a program needn't handle non-finite values.
Results may differ from the reference program's by a relative error of at most 0.00028.
Values sent between devices are 32-bit elements; how exact they have to be, the bound alone decides.
A program may use at most 64 MiB of HBM per device.

```python
import math
import jax
import jax.numpy as jnp
from jax import lax

B = 128
R = 256
LDEV = 12
NT = 4
P_SIZE = 2
LEAVES = 192
N_COLS = 2
N_LAYERS = 4


def draw_bottom_pivot_reciprocal(key, part):
    key_diag, key_off = jax.random.split(jax.random.fold_in(key, 11))
    diag_scale = jax.random.uniform(key_diag, (LEAVES, B, 1), jnp.float32, 0.7, 1.3)
    identity = (jnp.arange(B)[:, None] == jnp.arange(B)[None, :]).astype(jnp.float32)
    off_diag = jax.random.normal(key_off, (LEAVES, B, B), jnp.float32) * (0.4 / math.sqrt(B))
    return identity * diag_scale + off_diag


def draw_top_inv(key, part):
    key_diag, key_off = jax.random.split(jax.random.fold_in(key, 23))
    diag_scale = jax.random.uniform(key_diag, (NT, B, 1), jnp.float32, 0.7, 1.3)
    identity = (jnp.arange(B)[:, None] == jnp.arange(B)[None, :]).astype(jnp.float32)
    off_diag = jax.random.normal(key_off, (NT, B, B), jnp.float32) * (0.4 / math.sqrt(B))
    return identity * diag_scale + off_diag


def pick_row(random_seed_entry):
    return jax.random.permutation(random_seed_entry, NT)[:P_SIZE].astype(jnp.int32)


def draw_leaf_target(key, part):
    row_keys = jax.random.split(jax.random.fold_in(key, 37), LEAVES)
    return jax.vmap(pick_row)(row_keys)


def shard_levels(own_key, dims, cuts, least, largest):
    gain = 1.0
    for dim, shards_of in cuts:
        draws = jax.random.uniform(jax.random.fold_in(jax.random.fold_in(own_key, 6), dim), (shards_of,), jnp.float32, least / len(cuts), largest / len(cuts))
        gain = gain * jnp.repeat(jnp.exp(draws), dims[dim] // shards_of).reshape((-1,) + (1,) * (len(dims) - 1 - dim))
    return gain


def gaussian(stream_key, shape, spread, bound, cuts=(), kind=jnp.bfloat16):
    values = jax.random.normal(stream_key, shape, jnp.float32) * spread
    if len(cuts) > 0:
        values = shard_levels(stream_key, shape, cuts, -0.22, 0.18) * values
    return jnp.clip(values, min=-bound, max=bound).astype(kind)


def setup_inputs(seed: int = 0) -> dict:
    seeds = jax.random.split(jax.random.key(seed), 8)
    return {
        "bottom_known_vector": gaussian(seeds[0], (LEAVES, B, R), 1.0, 6.0, ((0, 16),), jnp.float32),
        "bottom_pivot_reciprocal": draw_bottom_pivot_reciprocal(jax.random.fold_in(seeds[7], 71), 0),
        "leaf_blocks": gaussian(seeds[2], (LEAVES, P_SIZE, B, B), (B * LDEV * N_LAYERS * N_COLS) ** -0.5, 0.0546875, ((0, 16), (1, 2)), jnp.float32),
        "leaf_target": draw_leaf_target(jax.random.fold_in(seeds[7], 71), 0),
        "top_rhs": gaussian(seeds[4], (NT, B, R), 1.0, 6.0, ((0, 4),), jnp.float32),
        "top_inv": draw_top_inv(jax.random.fold_in(seeds[7], 71), 0),
        "top_sub": gaussian(seeds[6], (NT, B, B), (B * 3 // 2) ** -0.5, 0.4375, ((0, 4),), jnp.float32),
    }


def reference(bottom_known_vector, bottom_pivot_reciprocal, leaf_blocks, leaf_target, top_rhs, top_inv, top_sub):
    exact_arithmetic_mode = lax.Precision.HIGHEST
    leaf_forward = jnp.einsum('jab,jbr->jar', bottom_pivot_reciprocal, bottom_known_vector, precision=exact_arithmetic_mode)

    def propagate_update(summed, leaf_item):
        blocks, solved, targets = leaf_item
        contrib = jnp.einsum('pab,br->par', blocks, solved, precision=exact_arithmetic_mode)
        return summed.at[targets].add(contrib), None

    carried, unused = lax.scan(propagate_update, jnp.zeros((NT, B, R), jnp.float32), (leaf_blocks, leaf_forward, leaf_target))

    def forward_step(previous, top_item):
        diag_inv, rhs_part, coupling = top_item
        solved = jnp.dot(diag_inv, rhs_part - jnp.dot(coupling, previous, precision=exact_arithmetic_mode), precision=exact_arithmetic_mode)
        return solved, solved

    start_zero = jnp.zeros((B, R), jnp.float32)
    unused_last, top_forward = lax.scan(forward_step, start_zero, (top_inv, top_rhs - carried, top_sub))
    coupling_next = jnp.concatenate([top_sub[1:], jnp.zeros((1, B, B), jnp.float32)], axis=0)

    def backward_step(following, top_item):
        diag_inv, forward_portion, coupling = top_item
        solved = jnp.dot(diag_inv.T, forward_portion - jnp.dot(coupling.T, following, precision=exact_arithmetic_mode), precision=exact_arithmetic_mode)
        return solved, solved

    unused_first, top_solution = lax.scan(backward_step, start_zero, (top_inv, top_forward, coupling_next), reverse=True)

    def leaf_step(leaf_item):
        diag_inv, blocks, solved, targets = leaf_item
        picked = top_solution[targets]
        back_sum = jnp.einsum('pab,par->br', blocks, picked, precision=exact_arithmetic_mode)
        return jnp.dot(diag_inv.T, solved - back_sum, precision=exact_arithmetic_mode)

    leaf_solution = lax.map(leaf_step, (bottom_pivot_reciprocal, leaf_blocks, leaf_forward, leaf_target))
    return leaf_solution, top_solution
```

```python
import functools

import jax
import jax.numpy as jnp
from jax import lax
from jax.experimental import pallas as pl
from jax.experimental.pallas import tpu as pltpu
from jax.sharding import PartitionSpec as P

F32 = jnp.float32
BF16 = jnp.bfloat16
MESH = pl.DeviceIdType.MESH
LANES = 128


def split(x):
    high = x.astype(BF16)
    low = (x - high.astype(F32)).astype(BF16)
    return high, low


def mul(a, b, rhs_transposed=False):
    (a_high, a_low), (b_high, b_low) = a, b
    axis = 1 if rhs_transposed else 0
    dot = functools.partial(
        lax.dot_general,
        dimension_numbers=(((1,), (axis,)), ((), ())),
        preferred_element_type=F32,
    )
    both = dot(
        jnp.concatenate([a_high, a_low], axis=1), jnp.concatenate([b_high, b_high], axis=axis)
    )
    return both + dot(a_high, b_low)


def peer_of(axis, stride, size, offset):
    index = lax.axis_index(axis)
    place = lax.rem(lax.div(index, stride), size)
    other = lax.rem(place + offset, size)
    return {axis: index + (other - place) * stride}, place, other


def kernel(
    sizes,
    known,
    pivot,
    blocks,
    target,
    top_rhs,
    top_inv,
    top_sub,
    out,
    top_out,
    pivot_full,
    pivot_turned,
    product,
    products,
    targets,
    inv_all,
    sub_all,
    forward_map,
    back_map,
    weights_high,
    weights_low,
    acc,
    full,
    sol,
    *rest,
):
    stages, chunks = sizes
    n_stage = len(stages)
    recv = rest[:n_stage]
    (pivot_sems, product_sems, target_sems, top_sems, sol_sems) = rest[n_stage : n_stage + 5]
    rs_sems = rest[n_stage + 5 : 2 * n_stage + 5]
    ag_sems = rest[2 * n_stage + 5 :]

    n_leaf, b, r = known.shape
    part = pivot.shape[1]
    n_cols = lax.axis_size("cols")
    n_rows = lax.axis_size("rows")
    halves = r // LANES
    col = lax.axis_index("cols")
    row = lax.axis_index("rows")
    layer = lax.axis_index("layers")
    per = n_leaf // chunks
    own_rows = pl.multiple_of(col * part, part)
    sent = []

    barrier = pltpu.get_barrier_semaphore()
    greeted = 0
    for axis, stride, size in stages:
        for offset in range(1, size):
            peer, _, _ = peer_of(axis, stride, size, offset)
            pl.semaphore_signal(barrier, inc=1, device_id=peer, device_id_type=MESH)
            greeted += 1
    pl.semaphore_wait(barrier, greeted)

    def remote(src, dst, sems, slot, peer):
        return pltpu.make_async_remote_copy(
            src_ref=src,
            dst_ref=dst,
            send_sem=sems.at[(0, *slot)],
            recv_sem=sems.at[(1, *slot)],
            device_id=peer,
            device_id_type=MESH,
        )

    def pivot_copy(offset, chunk):
        peer, _, _ = peer_of("cols", 1, n_cols, offset)
        leaves = pl.ds(chunk * per, per)
        return remote(
            pivot.at[leaves],
            pivot_full.at[leaves, pl.ds(own_rows, part), :],
            pivot_sems,
            (offset - 1, chunk),
            peer,
        )

    for chunk in range(chunks):
        for offset in range(1, n_cols):
            copy = pivot_copy(offset, chunk)
            copy.start()
            sent.append(copy)

    target_copies = []
    for offset in range(1, n_cols):
        peer, _, _ = peer_of("cols", 1, n_cols, offset)
        copy = remote(target, targets.at[col], target_sems, (offset - 1,), peer)
        copy.start()
        target_copies.append(copy)
    sent += target_copies

    top_copies = []
    for offset in range(1, n_rows):
        peer, _, _ = peer_of("rows", 1, n_rows, offset)
        for which, (src, dst) in enumerate(((top_inv, inv_all), (top_sub, sub_all))):
            copy = remote(src.at[0], dst.at[row], top_sems, (which, offset - 1), peer)
            copy.start()
            top_copies.append(copy)
    sent += top_copies

    inv_all[row] = top_inv[0]
    sub_all[row] = top_sub[0]
    targets[col] = target[...]

    n_top = n_rows
    per_half = n_top * b
    first = jnp.logical_and(col == 0, layer == 0)
    for h in range(halves):
        for t in range(n_top):
            mine = jnp.logical_and(first, row == t).astype(F32)
            acc[pl.ds(h * per_half + t * b, b), :] = (
                top_rhs[0, :, h * LANES : (h + 1) * LANES] * mine
            )

    def leaf_work(leaf):
        pivot_full[leaf, pl.ds(own_rows, part), :] = pivot[leaf]
        whole = pivot_full[leaf]
        rhs = split(known[leaf])
        block = split(blocks[leaf, 0])
        solved = split(mul(split(whole), rhs))
        contrib = mul(block, solved)
        which = target[pl.ds(leaf, 1), :]
        for t in range(n_top):
            mask = jnp.broadcast_to(which == t, (b, LANES))
            for h in range(halves):
                rows = pl.ds(h * per_half + t * b, b)
                acc[rows, :] = acc[rows, :] - jnp.where(
                    mask, contrib[:, h * LANES : (h + 1) * LANES], 0.0
                )
        turned = whole.T
        pivot_turned[leaf] = turned
        product[leaf] = mul(split(turned), block, rhs_transposed=True)
        out[leaf] = mul(split(pivot_turned[leaf, pl.ds(own_rows, part), :]), solved)

    def chunk_work(chunk, carry):
        for offset in range(1, n_cols):
            pivot_copy(offset, chunk).wait_recv()
        for i in range(per):
            leaf_work(chunk * per + i)
        return carry

    lax.fori_loop(0, chunks, chunk_work, 0)

    starts = [0]
    spans = [acc.shape[0]]

    def share(stage):
        return pl.ds(pl.multiple_of(starts[stage], 8), spans[stage])

    def reduce_start(stage):
        axis, stride, size = stages[stage]
        span = spans[-1] // size
        copies = []
        place = None
        for offset in range(1, size):
            peer, place, other = peer_of(axis, stride, size, offset)
            source = pl.ds(pl.multiple_of(starts[-1] + other * span, 8), span)
            copy = remote(
                acc.at[source], recv[stage].at[offset - 1], rs_sems[stage], (offset - 1,), peer
            )
            copy.start()
            copies.append(copy)
        if place is not None:
            starts.append(starts[-1] + place * span)
        else:
            starts.append(starts[-1])
        spans.append(span)
        return copies

    def reduce_end(stage, copies):
        rows = share(stage + 1)
        total = acc[rows, :]
        for i, copy in enumerate(copies):
            copy.wait_recv()
            total = total + recv[stage][i]
        if stage == n_stage - 1:
            full[rows, :] = total
        else:
            acc[rows, :] = total
        sent.extend(copies)

    def gather_start(buffer, stage, sems):
        axis, stride, size = stages[stage]
        rows = share(stage + 1)
        copies = []
        for offset in range(1, size):
            peer, _, _ = peer_of(axis, stride, size, offset)
            copy = remote(buffer.at[rows], buffer.at[rows], sems, (offset - 1,), peer)
            copy.start()
            copies.append(copy)
        return copies

    def landed(copies):
        for copy in copies:
            copy.wait_recv()
        sent.extend(copies)

    for stage in (0, 1):
        reduce_end(stage, reduce_start(stage))

    product_copies = []
    for offset in range(1, n_cols):
        peer, _, other = peer_of("cols", 1, n_cols, offset)
        rows = pl.ds(pl.multiple_of(other * part, part), part)
        copy = remote(
            product.at[:, rows, :], products.at[col], product_sems, (offset - 1,), peer
        )
        copy.start()
        product_copies.append(copy)

    copies = reduce_start(2)
    for copy in top_copies:
        copy.wait_recv()
    for t in range(n_top):
        inv = inv_all[t]
        if t > 0:
            forward_map[t] = -mul(split(inv), split(sub_all[t]))
        if t < n_top - 1:
            back_map[t] = -mul(split(inv.T), split(sub_all[t + 1]), rhs_transposed=True)
    reduce_end(2, copies)

    reduce_end(3, reduce_start(3))
    landed(gather_start(full, 3, ag_sems[3]))
    copies = gather_start(full, 2, ag_sems[2])
    landed(copies)
    copies = gather_start(full, 1, ag_sems[1])

    for copy in product_copies + target_copies:
        copy.wait_recv()
    sent += product_copies
    products[col] = product[:, pl.ds(own_rows, part), :]

    def weigh(leaf, carry):
        rows = pl.ds(pl.multiple_of(leaf * part, part), part)
        for t in range(n_top):
            value = jnp.zeros((part, b), F32)
            for c in range(n_cols):
                mask = jnp.broadcast_to(targets[c, pl.ds(leaf, 1), :] == t, (part, b))
                value = jnp.where(mask, -products[c, leaf], value)
            high, low = split(value)
            weights_high[rows, t * b : (t + 1) * b] = high
            weights_low[rows, t * b : (t + 1) * b] = low
        return carry

    lax.fori_loop(0, n_leaf, weigh, 0)
    landed(copies)

    own = pl.multiple_of(starts[1], 8)

    def rows_of(t):
        return pl.ds(pl.multiple_of(own + t * b, 8), b)

    current = None
    ahead = []
    for t in range(n_top):
        local = mul(split(inv_all[t]), split(full[rows_of(t), :]))
        if t > 0:
            local = local + mul(split(forward_map[t]), split(current))
        current = local
        ahead.append(mul(split(inv_all[t].T), split(current)))
    current = None
    for t in reversed(range(n_top)):
        value = ahead[t]
        if t < n_top - 1:
            value = value + mul(split(back_map[t]), split(current))
        current = value
        sol[rows_of(t), :] = value
    copies = gather_start(sol, 0, sol_sems)

    def finish(half):
        start = pl.multiple_of(half * per_half, 8)
        high, low = split(sol[pl.ds(start, per_half), :])
        lanes = pl.ds(pl.multiple_of(half * LANES, LANES), LANES)
        for leaf in range(0, n_leaf, 4):
            rows = slice(leaf * part, (leaf + 4) * part)
            dot = functools.partial(jnp.dot, preferred_element_type=F32)
            w_high, w_low = weights_high[rows, :], weights_low[rows, :]
            update = dot(w_high, high) + dot(w_low, high) + dot(w_high, low)
            for i in range(4):
                out[leaf + i, :, lanes] = (
                    out[leaf + i, :, lanes] + update[i * part : (i + 1) * part]
                )
        mine = pl.ds(pl.multiple_of(start + row * b, 8), b)
        top_out[0, :, lanes] = sol[mine, :]

    own_half = lax.rem(layer, 2)
    finish(own_half)
    landed(copies)
    finish(1 - own_half)

    for copy in sent:
        copy.wait_send()


def on_device(known, pivot, blocks, leaf_target, top_rhs, top_inv, top_sub):
    n_leaf, b, r = known.shape
    part = pivot.shape[1]
    n_rows, n_cols, n_layers = (lax.axis_size(a) for a in ("rows", "cols", "layers"))
    n_top = n_rows
    halves = r // LANES
    stages = (
        ("layers", 1, 2),
        ("cols", 1, n_cols),
        ("layers", 2, n_layers // 2),
        ("rows", 1, n_rows),
    )
    chunks = 4
    padded = -(-n_leaf // 8) * 8
    target = jnp.broadcast_to(
        jnp.pad(leaf_target, ((0, padded - n_leaf), (0, 0))), (padded, LANES)
    )
    total = halves * n_top * b
    spans = []
    span = total
    for _, _, size in stages:
        span //= size
        spans.append(span)
    dma = pltpu.SemaphoreType.DMA
    peers = [max(size - 1, 1) for _, _, size in stages]
    vmem = pl.BlockSpec(memory_space=pltpu.VMEM)
    return pl.pallas_call(
        functools.partial(kernel, (stages, chunks)),
        out_shape=(
            jax.ShapeDtypeStruct((n_leaf, part, r), F32),
            jax.ShapeDtypeStruct((1, b, r), F32),
        ),
        in_specs=[vmem] * 7,
        out_specs=(vmem, vmem),
        scratch_shapes=[
            pltpu.VMEM((n_leaf, b, b), F32),
            pltpu.VMEM((n_leaf, b, b), F32),
            pltpu.VMEM((n_leaf, b, b), F32),
            pltpu.VMEM((n_cols, n_leaf, part, b), F32),
            pltpu.VMEM((n_cols, padded, LANES), jnp.int32),
            pltpu.VMEM((n_top, b, b), F32),
            pltpu.VMEM((n_top, b, b), F32),
            pltpu.VMEM((n_top, b, b), F32),
            pltpu.VMEM((n_top, b, b), F32),
            pltpu.VMEM((n_leaf * part, n_top * b), BF16),
            pltpu.VMEM((n_leaf * part, n_top * b), BF16),
            pltpu.VMEM((total, LANES), F32),
            pltpu.VMEM((total, LANES), F32),
            pltpu.VMEM((total, LANES), F32),
            *[pltpu.VMEM((n, s, LANES), F32) for n, s in zip(peers, spans)],
            dma((2, max(n_cols - 1, 1), chunks)),
            dma((2, max(n_cols - 1, 1))),
            dma((2, max(n_cols - 1, 1))),
            dma((2, 2, max(n_rows - 1, 1))),
            dma((2, 1)),
            *[dma((2, n)) for n in peers],
            *[dma((2, n)) for n in peers],
        ],
        compiler_params=pltpu.CompilerParams(
            collective_id=0, has_side_effects=True, vmem_limit_bytes=48 * 1024 * 1024
        ),
    )(known, pivot, blocks, target, top_rhs, top_inv, top_sub)


def solution(mesh):
    in_specs = (
        P(("rows", "layers"), None, None),
        P(("rows", "layers"), "cols", None),
        P(("rows", "layers"), "cols", None, None),
        P(("rows", "layers"), "cols"),
        P("rows", None, None),
        P("rows", None, None),
        P("rows", None, None),
    )
    out_specs = (P(("rows", "layers"), "cols", None), P("rows", None, None))
    return jax.shard_map(
        on_device, mesh=mesh, in_specs=in_specs, out_specs=out_specs, check_vma=False
    )
```

```python
import functools

import jax
import jax.numpy as jnp
from jax import lax
from jax.experimental import pallas as pl
from jax.experimental.pallas import tpu as pltpu
from jax.sharding import PartitionSpec as P

F32 = jnp.float32
BF16 = jnp.bfloat16
MESH = pl.DeviceIdType.MESH
LANES = 128


def split(x):
    high = x.astype(BF16)
    low = (x - high.astype(F32)).astype(BF16)
    return high, low


def mul(a, b, rhs_transposed=False):
    (a_high, a_low), (b_high, b_low) = a, b
    axis = 1 if rhs_transposed else 0
    dot = functools.partial(
        lax.dot_general,
        dimension_numbers=(((1,), (axis,)), ((), ())),
        preferred_element_type=F32,
    )
    if a_high.shape[1] > 128:
        return dot(a_high, b_high) + dot(a_low, b_high) + dot(a_high, b_low)
    both = dot(
        jnp.concatenate([a_high, a_low], axis=1), jnp.concatenate([b_high, b_high], axis=axis)
    )
    return both + dot(a_high, b_low)


def group_size(stage):
    total = 1
    for _, _, size in stage:
        total *= size
    return total


def peer_of(stage, offset):
    device, place, other = {}, 0, 0
    for axis, stride, size in stage:
        offset, digit = divmod(offset, size)
        index = lax.axis_index(axis)
        mine = lax.rem(lax.div(index, stride), size)
        theirs = lax.rem(mine + digit, size)
        if size > 1:
            device[axis] = index + (theirs - mine) * stride
        place = place * size + mine
        other = other * size + theirs
    return device, place, other


def kernel(
    sizes,
    known_hbm,
    pivot,
    blocks_hbm,
    target_smem,
    rhs_hbm,
    top_inv,
    top_sub,
    out,
    top_out,
    known,
    blocks,
    target,
    top_rhs,
    pivot_full,
    pivot_turned,
    solved_high,
    solved_low,
    product,
    products,
    targets,
    inv_all,
    sub_all,
    forward_map,
    back_map,
    lower_high,
    lower_low,
    inverse_high,
    inverse_low,
    weights_high,
    weights_low,
    acc,
    full,
    sol,
    *rest,
):
    stages, chunks = sizes
    n_stage = len(stages)
    recv = rest[:n_stage]
    (local_sems, pivot_sems, product_sems, target_sems, top_sems, sol_sems) = rest[
        n_stage : n_stage + 6
    ]
    rs_sems = rest[n_stage + 6 : 2 * n_stage + 6]
    ag_sems = rest[2 * n_stage + 6 :]

    n_leaf, b, r = known.shape
    part = pivot.shape[1]
    n_cols = lax.axis_size("cols")
    n_rows = lax.axis_size("rows")
    n_top = n_rows
    halves = r // LANES
    col = lax.axis_index("cols")
    row = lax.axis_index("rows")
    layer = lax.axis_index("layers")
    per = n_leaf // chunks
    own_rows = pl.multiple_of(col * part, part)
    cols_stage = (("cols", 1, n_cols),)
    rows_stage = (("rows", 1, n_rows),)
    sent = []

    barrier = pltpu.get_barrier_semaphore()
    greeted = 0
    for stage in stages:
        for offset in range(1, group_size(stage)):
            peer, _, _ = peer_of(stage, offset)
            pl.semaphore_signal(barrier, inc=1, device_id=peer, device_id_type=MESH)
            greeted += 1

    loads = [
        pltpu.make_async_copy(src, dst, local_sems.at[i])
        for i, (src, dst) in enumerate(
            (
                (pivot, pivot_full.at[:, pl.ds(own_rows, part), :]),
                (known_hbm, known),
                (blocks_hbm.at[:, 0], blocks),
                (rhs_hbm.at[0], top_rhs),
                (top_inv.at[0], inv_all.at[row]),
                (top_sub.at[0], sub_all.at[row]),
            )
        )
    ]
    for copy in loads:
        copy.start()
    for leaf in range(n_leaf):
        target[leaf : leaf + 1, :] = jnp.full((1, LANES), target_smem[leaf, 0], jnp.int32)
    for leaf in range(n_leaf, target.shape[0]):
        target[leaf : leaf + 1, :] = jnp.zeros((1, LANES), jnp.int32)
    targets[col] = target[...]
    pl.semaphore_wait(barrier, greeted)

    def remote(src, dst, sems, slot, peer):
        return pltpu.make_async_remote_copy(
            src_ref=src,
            dst_ref=dst,
            send_sem=sems.at[(0, *slot)],
            recv_sem=sems.at[(1, *slot)],
            device_id=peer,
            device_id_type=MESH,
        )

    def pivot_copy(offset, chunk):
        peer, _, _ = peer_of(cols_stage, offset)
        leaves = pl.ds(chunk * per, per)
        return remote(
            pivot.at[leaves],
            pivot_full.at[leaves, pl.ds(own_rows, part), :],
            pivot_sems,
            (offset - 1, chunk),
            peer,
        )

    for chunk in range(chunks):
        for offset in range(1, n_cols):
            copy = pivot_copy(offset, chunk)
            copy.start()
            sent.append(copy)

    target_copies = []
    for offset in range(1, n_cols):
        peer, _, _ = peer_of(cols_stage, offset)
        copy = remote(target, targets.at[col], target_sems, (offset - 1,), peer)
        copy.start()
        target_copies.append(copy)
    sent += target_copies

    top_copies = []
    for offset in range(1, n_rows):
        peer, _, _ = peer_of(rows_stage, offset)
        for which, (src, dst) in enumerate(((top_inv, inv_all), (top_sub, sub_all))):
            copy = remote(src.at[0], dst.at[row], top_sems, (which, offset - 1), peer)
            copy.start()
            top_copies.append(copy)
    sent += top_copies

    for copy in loads:
        copy.wait()

    per_half = n_top * b
    first = jnp.logical_and(col == 0, layer == 0)
    for h in range(halves):
        for t in range(n_top):
            mine = jnp.logical_and(first, row == t).astype(F32)
            acc[pl.ds(h * per_half + t * b, b), :] = (
                top_rhs[:, h * LANES : (h + 1) * LANES] * mine
            )

    def forward_work(chunk):
        for offset in range(1, n_cols):
            pivot_copy(offset, chunk).wait_recv()
        contribs, picks = [], []
        for i in range(per):
            leaf = chunk * per + i
            solved = split(mul(split(pivot_full[leaf]), split(known[leaf])))
            solved_high[i], solved_low[i] = solved
            contribs.append(mul(split(blocks[leaf]), solved))
            picks.append(target[pl.ds(leaf, 1), :])
        for t in range(n_top):
            masks = [jnp.broadcast_to(pick == t, (b, LANES)) for pick in picks]
            for h in range(halves):
                rows = pl.ds(h * per_half + t * b, b)
                total = acc[rows, :]
                for mask, contrib in zip(masks, contribs):
                    total = total - jnp.where(
                        mask, contrib[:, h * LANES : (h + 1) * LANES], 0.0
                    )
                acc[rows, :] = total

    def later_work(chunk):
        for i in range(per):
            leaf = chunk * per + i
            turned = pivot_full[leaf].T
            pivot_turned[leaf] = turned
            product[leaf] = mul(split(turned), split(blocks[leaf]), rhs_transposed=True)
            own = split(pivot_turned[leaf, pl.ds(own_rows, part), :])
            out[leaf] = mul(own, (solved_high[i], solved_low[i]))

    def chunk_work(chunk, carry):
        forward_work(chunk)
        later_work(chunk)
        return carry

    lax.fori_loop(0, chunks - 1, chunk_work, 0)
    forward_work(chunks - 1)

    starts = [0]
    spans = [acc.shape[0]]

    def share(stage):
        return pl.ds(pl.multiple_of(starts[stage], 8), spans[stage])

    def reduce_start(stage):
        size = group_size(stages[stage])
        span = spans[-1] // size
        copies = []
        for offset in range(1, size):
            peer, _, other = peer_of(stages[stage], offset)
            source = pl.ds(pl.multiple_of(starts[-1] + other * span, 8), span)
            copy = remote(
                acc.at[source], recv[stage].at[offset - 1], rs_sems[stage], (offset - 1,), peer
            )
            copy.start()
            copies.append(copy)
        _, place, _ = peer_of(stages[stage], 0)
        starts.append(starts[-1] + place * span)
        spans.append(span)
        return copies

    def reduce_end(stage, copies):
        rows = share(stage + 1)
        total = acc[rows, :]
        for i, copy in enumerate(copies):
            copy.wait_recv()
            total = total + recv[stage][i]
        if stage == n_stage - 1:
            full[rows, :] = total
        else:
            acc[rows, :] = total
        sent.extend(copies)

    def gather_start(buffer, stage, sems):
        rows = share(stage + 1)
        copies = []
        for offset in range(1, group_size(stages[stage])):
            peer, _, _ = peer_of(stages[stage], offset)
            copy = remote(buffer.at[rows], buffer.at[rows], sems, (offset - 1,), peer)
            copy.start()
            copies.append(copy)
        return copies

    def landed(copies):
        for copy in copies:
            copy.wait_recv()
        sent.extend(copies)

    def each(first, last, body):
        if n_top <= 4:
            for t in range(first, last):
                body(t)
        else:
            lax.fori_loop(first, last, lambda t, carry: (body(t), carry)[1], 0)

    def rows_at(t, start=0):
        return pl.ds(pl.multiple_of(start + t * b, 8), b)

    copies = reduce_start(0)
    later_work(chunks - 1)
    reduce_end(0, copies)
    copies = reduce_start(1)

    for copy in top_copies:
        copy.wait_recv()

    def forward_step(t):
        forward_map[t] = -mul(split(inv_all[t]), split(sub_all[t]))

    def back_step(t):
        back_map[t] = -mul(split(inv_all[t].T), split(sub_all[t + 1]), rhs_transposed=True)

    def lower_step(t):
        before = rows_at(t - 1)
        value = mul(split(forward_map[t]), (lower_high[before, :], lower_low[before, :]))
        lower_high[rows_at(t), :], lower_low[rows_at(t), :] = split(value)
        place_inverse(t)

    def place_inverse(t):
        lanes = pl.ds(pl.multiple_of(t * b, b), b)
        high, low = split(inv_all[t])
        lower_high[rows_at(t), lanes] = high
        lower_low[rows_at(t), lanes] = low

    def inverse_step(i):
        t = n_top - 1 - i
        here, after = rows_at(t), rows_at(t + 1)
        value = mul(split(inv_all[t].T), (lower_high[here, :], lower_low[here, :]))
        if not (isinstance(i, int) and i == 0):
            value = value + mul(
                split(back_map[t]), (inverse_high[after, :], inverse_low[after, :])
            )
        inverse_high[here, :], inverse_low[here, :] = split(value)

    each(1, n_top, forward_step)
    each(0, n_top - 1, back_step)
    reduce_end(1, copies)

    product_copies = []
    for offset in range(1, n_cols):
        peer, _, other = peer_of(cols_stage, offset)
        rows = pl.ds(pl.multiple_of(other * part, part), part)
        copy = remote(
            product.at[:, rows, :], products.at[col], product_sems, (offset - 1,), peer
        )
        product_copies.append(copy)

    copies = reduce_start(2)
    for copy in product_copies:
        copy.start()
    lower_high[0:b, :] = jnp.zeros((b, n_top * b), BF16)
    lower_low[0:b, :] = jnp.zeros((b, n_top * b), BF16)
    place_inverse(0)
    each(1, n_top, lower_step)
    reduce_end(2, copies)
    copies = gather_start(full, 2, ag_sems[2])
    inverse_step(0)
    each(1, n_top, inverse_step)
    landed(copies)
    copies = gather_start(full, 1, ag_sems[1])

    for copy in product_copies + target_copies:
        copy.wait_recv()
    sent += product_copies
    products[col] = product[:, pl.ds(own_rows, part), :]

    def weigh(leaf, carry):
        rows = pl.ds(pl.multiple_of(leaf * part, part), part)
        for t in range(n_top):
            value = jnp.zeros((part, b), F32)
            for c in range(n_cols):
                mask = jnp.broadcast_to(targets[c, pl.ds(leaf, 1), :] == t, (part, b))
                value = jnp.where(mask, -products[c, leaf], value)
            high, low = split(value)
            weights_high[rows, t * b : (t + 1) * b] = high
            weights_low[rows, t * b : (t + 1) * b] = low
        return carry

    lax.fori_loop(0, n_leaf, weigh, 0)
    landed(copies)

    own = pl.multiple_of(starts[1], 8)
    right = split(full[pl.ds(own, per_half), :])

    def solve_rows(t):
        here = rows_at(t)
        sol[rows_at(t, own), :] = mul((inverse_high[here, :], inverse_low[here, :]), right)

    each(0, n_top, solve_rows)
    copies = gather_start(sol, 0, sol_sems)

    def finish(half):
        start = pl.multiple_of(half * per_half, 8)
        high, low = split(sol[pl.ds(start, per_half), :])
        lanes = pl.ds(pl.multiple_of(half * LANES, LANES), LANES)
        for leaf in range(0, n_leaf, 4):
            rows = slice(leaf * part, (leaf + 4) * part)
            dot = functools.partial(jnp.dot, preferred_element_type=F32)
            w_high, w_low = weights_high[rows, :], weights_low[rows, :]
            update = dot(w_high, high) + dot(w_low, high) + dot(w_high, low)
            for i in range(4):
                out[leaf + i, :, lanes] = (
                    out[leaf + i, :, lanes] + update[i * part : (i + 1) * part]
                )
        mine = pl.ds(pl.multiple_of(start + row * b, 8), b)
        top_out[0, :, lanes] = sol[mine, :]

    own_half = lax.rem(layer, 2)
    finish(own_half)
    landed(copies)
    finish(1 - own_half)

    for copy in sent:
        copy.wait_send()


def on_device(known, pivot, blocks, leaf_target, top_rhs, top_inv, top_sub):
    n_leaf, b, r = known.shape
    part = pivot.shape[1]
    n_rows, n_cols, n_layers = (lax.axis_size(a) for a in ("rows", "cols", "layers"))
    n_top = n_rows
    halves = r // LANES
    stages = (
        (("layers", 1, 2),),
        (("cols", 1, n_cols), ("layers", 2, n_layers // 2)),
        (("rows", 1, n_rows),),
    )
    chunks = 4
    padded = -(-n_leaf // 8) * 8
    total = halves * n_top * b
    spans = []
    span = total
    for stage in stages:
        span //= group_size(stage)
        spans.append(span)
    dma = pltpu.SemaphoreType.DMA
    peers = [max(group_size(stage) - 1, 1) for stage in stages]
    hbm = pl.BlockSpec(memory_space=pltpu.HBM)
    vmem = pl.BlockSpec(memory_space=pltpu.VMEM)
    return pl.pallas_call(
        functools.partial(kernel, (stages, chunks)),
        out_shape=(
            jax.ShapeDtypeStruct((n_leaf, part, r), F32),
            jax.ShapeDtypeStruct((1, b, r), F32),
        ),
        in_specs=[hbm, hbm, hbm, pl.BlockSpec(memory_space=pltpu.SMEM), hbm, hbm, hbm],
        out_specs=(vmem, vmem),
        scratch_shapes=[
            pltpu.VMEM((n_leaf, b, r), F32),
            pltpu.VMEM((n_leaf, b, b), F32),
            pltpu.VMEM((padded, LANES), jnp.int32),
            pltpu.VMEM((b, r), F32),
            pltpu.VMEM((n_leaf, b, b), F32),
            pltpu.VMEM((n_leaf, b, b), F32),
            pltpu.VMEM((n_leaf // chunks, b, r), BF16),
            pltpu.VMEM((n_leaf // chunks, b, r), BF16),
            pltpu.VMEM((n_leaf, b, b), F32),
            pltpu.VMEM((n_cols, n_leaf, part, b), F32),
            pltpu.VMEM((n_cols, padded, LANES), jnp.int32),
            pltpu.VMEM((n_top, b, b), F32),
            pltpu.VMEM((n_top, b, b), F32),
            pltpu.VMEM((n_top, b, b), F32),
            pltpu.VMEM((n_top, b, b), F32),
            *[pltpu.VMEM((n_top * b, n_top * b), BF16)] * 4,
            pltpu.VMEM((n_leaf * part, n_top * b), BF16),
            pltpu.VMEM((n_leaf * part, n_top * b), BF16),
            pltpu.VMEM((total, LANES), F32),
            pltpu.VMEM((total, LANES), F32),
            pltpu.VMEM((total, LANES), F32),
            *[pltpu.VMEM((n, s, LANES), F32) for n, s in zip(peers, spans)],
            dma((6,)),
            dma((2, max(n_cols - 1, 1), chunks)),
            dma((2, max(n_cols - 1, 1))),
            dma((2, max(n_cols - 1, 1))),
            dma((2, 2, max(n_rows - 1, 1))),
            dma((2, 1)),
            *[dma((2, n)) for n in peers],
            *[dma((2, n)) for n in peers],
        ],
        compiler_params=pltpu.CompilerParams(
            collective_id=0, has_side_effects=True, vmem_limit_bytes=60 * 1024 * 1024
        ),
    )(known, pivot, blocks, leaf_target, top_rhs, top_inv, top_sub)


def solution(mesh):
    in_specs = (
        P(("rows", "layers"), None, None),
        P(("rows", "layers"), "cols", None),
        P(("rows", "layers"), "cols", None, None),
        P(("rows", "layers"), "cols"),
        P("rows", None, None),
        P("rows", None, None),
        P("rows", None, None),
    )
    out_specs = (P(("rows", "layers"), "cols", None), P("rows", None, None))
    return jax.shard_map(
        on_device, mesh=mesh, in_specs=in_specs, out_specs=out_specs, check_vma=False
    )
```
